256 devices in a mesh: section: 4 (over x), tensor: 2 (over core), dp: 32 (over z, y).
Axes of the slice: x: 4, y: 4, z: 8, core: 2. Of those that a mesh axis runs over, the one named last changes fastest.
Arguments:
- inputs: bfloat16 [4, 4096, 8192], P('section', 'dp', 'tensor'), may hold values from -6 to 6
- segment_ids: int32 [4, 4096], P('section', 'dp'), may hold values from 0 to 127, never falling along the last dimension, each value on 1 to 64 neighbouring positions
- key_weight: bfloat16 [4, 8192, 512], P('section', ('tensor', 'dp')), may hold values from -0.049939416 to 0.049939416
- value_weight: bfloat16 [4, 8192, 512], P('section', ('tensor', 'dp')), may hold values from -0.0625 to 0.0625
- out_weight: bfloat16 [4, 512, 8192], P('section', 'dp', 'tensor'), may hold values from -0.25 to 0.25
- norm_gain: bfloat16 [4, 8192], P('section'), may hold values from 0.099609375 to 1.8984375
Outputs:
- final: bfloat16 [4, 4096, 8192], P('section', 'dp', 'tensor')
- backup: bfloat16 [4, 4096, 8192], P('section', 'dp', 'tensor')
The draws below stay inside these ranges and needn't reach their ends.
All inputs are finite; a program needn't handle non-finite values.
Results may differ from the reference program's by a relative error of at most 0.0095.
Values may be sent and summed in bfloat16 or wider, within the bound.
No kernel may reach another device: no remote copies, remote signals or barrier semaphores. Data moves between devices by JAX's collectives and lax.ppermute only.
A program may use at most 128 MiB of HBM per device.

```python
import math
import jax
import jax.numpy as jnp
import numpy as np
from jax import lax

D = 8192
HD = 128
HEADS = 4
ROWS = 128
SECTIONS = 4
BATCH_ROWS = 4096
N_DP = 32


def draw_inputs(key, part):
    key = jax.random.fold_in(key, 11)
    noise_key = jax.random.fold_in(key, 0)
    noise_rows = jax.random.normal(noise_key, (SECTIONS, BATCH_ROWS, D), jnp.float32)
    drawn_rows = jnp.clip(noise_rows, -4.5, 4.5)
    return drawn_rows.astype(jnp.bfloat16)


def draw_key_weight(key, part):
    key = jax.random.fold_in(key, 23)
    base_key = jax.random.fold_in(key, 0)
    base_values = jax.random.normal(base_key, (SECTIONS, D, HEADS * HD), jnp.float32)
    drawn_values = jnp.clip(base_values, -4.5, 4.5) / math.sqrt(D)
    return drawn_values.astype(jnp.bfloat16)


def levels(key, extent, pieces, low, largest):
    gain, own = 1.0, jax.random.fold_in(key, 6)
    for dim, blocks in pieces:
        heights = jnp.exp(jax.random.uniform(jax.random.fold_in(own, dim), (blocks,), jnp.float32, low / len(pieces), largest / len(pieces)))
        gain = gain * jnp.repeat(heights, extent[dim] // blocks).reshape([-1 if axis == dim else 1 for axis in range(len(extent))])
    return gain


def profile(amount, total, limit, lean):
    weights = [(1 << 20) // math.isqrt(grade ** lean) + 1 for grade in range(2, amount + 1)]
    spare, given = total - limit - (amount - 1), [1] * (amount - 1)
    while spare > 0:
        movable = [i for i in range(amount - 1) if given[i] < limit]
        whole, left = sum([weights[i] for i in movable]), spare
        for i in movable:
            more = min(limit - given[i], max(1, left * weights[i] // whole), spare)
            given[i] = given[i] + more
            spare = spare - more
    return np.array([limit] + given)


def uneven_parts(key, count, total, limit, lean):
    if count == 2:
        one = jax.random.randint(key, (), max(1, total - limit), min(limit, total - 1) + 1)
        return jnp.stack([one, total - one])
    sizes = jnp.asarray(profile(count, total, limit, lean), jnp.int32)
    couples = (count - 1) // 2
    source_of, receiver = sizes[1:1 + 2 * couples:2], sizes[2:2 + 2 * couples:2]
    margin = jnp.minimum(source_of - 1, limit - receiver)
    shifted = jax.random.randint(jax.random.fold_in(key, 1), (couples,), 0, 1 << 20) % (margin + 1)
    sizes = sizes.at[1:1 + 2 * couples:2].set(source_of - shifted).at[2:2 + 2 * couples:2].set(receiver + shifted)
    return sizes[jax.random.permutation(jax.random.fold_in(key, 2), count)]


def noise(stream_key, shape, width, bound, cuts=(), dtype=jnp.bfloat16):
    array = jax.random.normal(stream_key, shape, jnp.float32) * width
    if len(cuts) > 0:
        array = levels(stream_key, shape, cuts, -0.22, 0.18) * array
    return jnp.clip(array, min=-bound, max=bound).astype(dtype)


def setup_inputs(seed: int = 0) -> dict:
    arg_keys = jax.random.split(jax.random.key(seed), 7)
    return {
        "inputs": draw_inputs(jax.random.fold_in(arg_keys[6], 71), 0),
        "segment_ids": jax.vmap(lambda own: jnp.searchsorted(jnp.cumsum(uneven_parts(own, 4 * N_DP, BATCH_ROWS, ROWS // 2, 2)), jnp.arange(BATCH_ROWS), side="right"))(jax.random.split(arg_keys[1], SECTIONS)).reshape((SECTIONS, BATCH_ROWS)).astype(jnp.int32),
        "key_weight": draw_key_weight(jax.random.fold_in(arg_keys[6], 71), 0),
        "value_weight": noise(arg_keys[3], (SECTIONS, D, HEADS * HD), D ** -0.5, 0.0625, ((0, 4), (1, 64))),
        "out_weight": noise(arg_keys[4], (SECTIONS, HEADS * HD, D), (HEADS * HD) ** -0.5, 0.25, ((0, 4), (1, 32), (2, 2))),
        "norm_gain": jnp.clip(1.0 + 0.18 * jax.random.normal(arg_keys[5], (SECTIONS, D), jnp.float32), 0.099609375, 1.8984375).astype(jnp.bfloat16),
    }


def layer(row_block, seg_ids, w_key, w_value, w_out, gain_row):
    row_count = row_block.shape[0]
    blocks = row_count // ROWS
    wide_rows = row_block.astype(jnp.float32)
    scale_inv = lax.rsqrt(lax.optimization_barrier(jnp.sum(wide_rows * wide_rows, axis=1, keepdims=True)) / D + 1e-05)
    scaled = (wide_rows * gain_row.astype(jnp.float32)).astype(jnp.bfloat16)
    key_rows = (jnp.dot(scaled, w_key, preferred_element_type=jnp.float32) * scale_inv).astype(jnp.bfloat16)
    value_rows = (jnp.dot(scaled, w_value, preferred_element_type=jnp.float32) * scale_inv).astype(jnp.bfloat16)
    key_heads = key_rows.astype(jnp.float32).reshape(blocks, ROWS, HEADS, HD)
    value_heads = value_rows.astype(jnp.float32).reshape(blocks, ROWS, HEADS, HD)
    scores = jnp.einsum('bihd,bjhd->bhij', key_heads, key_heads) / HD
    position = jnp.arange(ROWS)
    seg_block = seg_ids.reshape(blocks, ROWS)
    allowed = (position[None, None, :] <= position[None, :, None]) & (seg_block[:, None, :] == seg_block[:, :, None])
    scores = jnp.where(allowed[:, None], scores, -1e+30)
    row_max = lax.optimization_barrier(jnp.max(scores, axis=3, keepdims=True))
    lifted = jnp.exp(scores - row_max)
    probs = (lifted / lax.optimization_barrier(jnp.sum(lifted, axis=3, keepdims=True))).astype(jnp.bfloat16)
    attended = jnp.einsum('bhij,bjhd->bihd', probs.astype(jnp.float32), value_heads).astype(jnp.bfloat16).reshape(row_count, HEADS * HD)
    mixed_rows = jnp.dot(attended, w_out, preferred_element_type=jnp.float32)
    return (wide_rows + mixed_rows).astype(jnp.bfloat16)

def run_sections(row_stack, seg_stack, key_stack, value_stack, out_stack, gain_stack):
    return lax.map(lambda items: layer(*items), (row_stack, seg_stack, key_stack, value_stack, out_stack, gain_stack))

def reference(inputs, segment_ids, key_weight, value_weight, out_weight, norm_gain):
    first_out = run_sections(inputs, segment_ids, key_weight, value_weight, out_weight, norm_gain)
    prev_rows = jnp.roll(first_out, 1, axis=0)
    prev_segs = jnp.roll(segment_ids, 1, axis=0)
    final_out = run_sections(prev_rows, prev_segs, key_weight, value_weight, out_weight, norm_gain)
    backup_out = run_sections(final_out, prev_segs, jnp.roll(key_weight, -1, axis=0), jnp.roll(value_weight, -1, axis=0), jnp.roll(out_weight, -1, axis=0), jnp.roll(norm_gain, -1, axis=0))
    return (final_out, backup_out)
```

```python
import functools

import jax
import jax.numpy as jnp
from jax import lax
from jax.experimental import pallas as pl
from jax.experimental.pallas import tpu as pltpu
from jax.sharding import Mesh
from jax.sharding import PartitionSpec as P

D = 8192
HD = 128
ROWS = 128
HALF = 4096
CHUNKS = 4
F32 = jnp.float32
BF16 = jnp.bfloat16
ANY = pl.BlockSpec(memory_space=pl.ANY)
VMEM = pl.BlockSpec(memory_space=pltpu.VMEM)
SMEM = pl.BlockSpec(memory_space=pltpu.SMEM)


def shift(block, axis, distance):
    n = lax.axis_size(axis)
    return lax.ppermute(block, axis, [(i, (i + distance) % n) for i in range(n)])


def place(buffer, block, *where):
    start = list(where) + [0] * (buffer.ndim - len(where))
    return lax.dynamic_update_slice(buffer, block, start)


def gather_weights(w_key, w_value, w_out):
    z, y = lax.axis_index("z"), lax.axis_index("y")
    w_out = w_out.reshape(16, 8, 512).transpose(1, 0, 2).reshape(128, 512)
    low = jnp.concatenate([w_key, w_out[:64]], axis=0)
    high = jnp.concatenate([w_value, w_out[64:]], axis=0)

    from_prev, from_next = shift(high, "y", 1), shift(high, "y", -1)
    far = jnp.concatenate([shift(from_prev[:96], "y", 1), shift(from_next[96:], "y", -1)], axis=0)
    value_y = jnp.zeros((4, 128, 512), BF16)
    outh_y = jnp.zeros((4, 64, 512), BF16)
    for block, offset in ((high, 0), (from_prev, 3), (from_next, 1), (far, 2)):
        at = (y + offset) % 4
        value_y = place(value_y, block[None, :128], at)
        outh_y = place(outh_y, block[None, 128:], at)

    key_z = place(jnp.zeros((8, 128, 512), BF16), low[None, :128], z)
    outl_z = place(jnp.zeros((8, 64, 512), BF16), low[None, 128:], z)
    up, down = low, low
    for step in range(1, 4):
        up, down = shift(up, "z", 1), shift(down, "z", -1)
        for block, offset in ((up, 8 - step), (down, step)):
            at = (z + offset) % 8
            key_z = place(key_z, block[None, :128], at)
            outl_z = place(outl_z, block[None, 128:], at)
    far = jnp.concatenate([shift(up[:96], "z", 1), shift(down[96:], "z", -1)], axis=0)
    key_z = place(key_z, far[None, :128], (z + 4) % 8)
    outl_z = place(outl_z, far[None, 128:], (z + 4) % 8)

    def over_z(own):
        out = place(jnp.zeros((8,) + own.shape, BF16), own[None], z)
        up, down = own, own
        for step in range(1, 4):
            up, down = shift(up, "z", 1), shift(down, "z", -1)
            out = place(out, up[None], (z + 8 - step) % 8)
            out = place(out, down[None], (z + step) % 8)
        out = place(out, shift(up[:2], "z", 1)[None], (z + 4) % 8, 0)
        return place(out, shift(down[2:], "z", -1)[None], (z + 4) % 8, 2)

    def over_y(own):
        out = place(jnp.zeros((8, 4) + own.shape[1:], BF16), own[:, None], 0, y)
        up, down = shift(own, "y", 1), shift(own, "y", -1)
        out = place(out, up[:, None], 0, (y + 3) % 4)
        out = place(out, down[:, None], 0, (y + 1) % 4)
        out = place(out, shift(up[:4], "y", 1)[:, None], 0, (y + 2) % 4)
        return place(out, shift(down[4:], "y", -1)[:, None], 4, (y + 2) % 4)

    return over_y(key_z), over_z(value_y), over_y(outl_z), over_z(outh_y)


def project_kernel(chunks, first, last, *refs):
    refs = list(refs)
    core = refs.pop(0)
    rows = [refs.pop(0) for _ in chunks]
    gain, key_hbm, value_hbm = refs.pop(0), refs.pop(0), refs.pop(0)
    before = None if first else refs.pop(0)
    outs = [refs.pop(0) for _ in range(2 if last else 1)]
    key_w, value_w, total, sems = refs

    copies = []
    for n, chunk in enumerate(chunks):
        part = pl.ds(2 * chunk, 2)
        copies.append(
            (
                pltpu.make_async_copy(key_hbm.at[part], key_w.at[n], sems.at[2 * n]),
                pltpu.make_async_copy(value_hbm.at[part], value_w.at[n], sems.at[2 * n + 1]),
            )
        )
    for pair in copies:
        for copy in pair:
            copy.start()
    if first:
        key_sum = jnp.zeros((ROWS, 512), F32)
        value_sum = jnp.zeros((ROWS, 512), F32)
        squares = jnp.zeros((ROWS, 1), F32)
    else:
        key_sum, value_sum = before[:, :512], before[:, 512:1024]
        squares = before[:, 1024:1025]
    for n, chunk in enumerate(chunks):
        wide = rows[n][...].astype(F32)
        squares = squares + jnp.sum(wide * wide, axis=1, keepdims=True)
        scaled = (wide * gain[:, chunk * 1024 : chunk * 1024 + 1024].astype(F32)).astype(BF16)
        copies[n][0].wait()
        key_sum += jnp.dot(scaled, key_w[n].reshape(1024, 512), preferred_element_type=F32)
        copies[n][1].wait()
        value_sum += jnp.dot(scaled, value_w[n].reshape(1024, 512), preferred_element_type=F32)
    spread = jnp.broadcast_to(squares, (ROWS, 128))
    if not last:
        outs[0][:, :512] = key_sum
        outs[0][:, 512:1024] = value_sum
        outs[0][:, 1024:] = spread
        return
    total[:, :512] = key_sum
    total[:, 512:] = value_sum
    for out, who in ((outs[0], core[0]), (outs[1], 1 - core[0])):
        out[:, :256] = total[:, pl.ds(pl.multiple_of(who * 256, 256), 256)]
        out[:, 256:512] = total[:, pl.ds(pl.multiple_of(512 + who * 256, 256), 256)]
        out[:, 512:] = spread


def project(core, chunks, rows, gain, w_key, w_value, before, last):
    first = before is None
    many = len(chunks)
    if last:
        shapes = [jax.ShapeDtypeStruct((ROWS, 640), F32)] * 2
    else:
        shapes = [jax.ShapeDtypeStruct((ROWS, 1152), F32)]
    return pl.pallas_call(
        functools.partial(project_kernel, chunks, first, last),
        out_shape=shapes,
        in_specs=[SMEM] + [VMEM] * many + [VMEM, ANY, ANY] + ([] if first else [VMEM]),
        out_specs=[VMEM] * len(shapes),
        scratch_shapes=[
            pltpu.VMEM((many, 2, 4, 128, 512), BF16),
            pltpu.VMEM((many, 2, 4, 128, 512), BF16),
            pltpu.VMEM((ROWS, 1024), F32),
            pltpu.SemaphoreType.DMA((2 * many,)),
        ],
        compiler_params=pltpu.CompilerParams(vmem_limit_bytes=40 * 2**20),
        cost_estimate=pl.CostEstimate(
            flops=many * 2 * 128 * 1024 * 1024, bytes_accessed=many * 2 * 2**20, transcendentals=0
        ),
        name="project",
    )(core, *rows, gain, w_key, w_value, *([] if first else [before]))


def attend_kernel(own, other, seg_row, seg_col, out):
    total = own[...] + other[...]
    scale = lax.rsqrt(total[:, 512:513] / D + 1e-05)
    keys = (total[:, :256] * scale).astype(BF16)
    values = (total[:, 256:512] * scale).astype(BF16)
    i = lax.broadcasted_iota(jnp.int32, (ROWS, ROWS), 0)
    j = lax.broadcasted_iota(jnp.int32, (ROWS, ROWS), 1)
    allowed = (j <= i) & (seg_row[...] == seg_col[...])
    for head in range(2):
        cols = slice(head * HD, head * HD + HD)
        k = keys[:, cols]
        scores = lax.dot_general(k, k, (((1,), (1,)), ((), ())), preferred_element_type=F32) / HD
        scores = jnp.where(allowed, scores, -1e30)
        lifted = jnp.exp(scores - jnp.max(scores, axis=1, keepdims=True))
        probs = (lifted / jnp.sum(lifted, axis=1, keepdims=True)).astype(BF16)
        out[:, cols] = jnp.dot(probs, values[:, cols], preferred_element_type=F32).astype(BF16)


def attend(own, other, seg):
    return pl.pallas_call(
        attend_kernel,
        out_shape=jax.ShapeDtypeStruct((ROWS, 256), BF16),
        in_specs=[VMEM] * 4,
        out_specs=VMEM,
        name="attend",
    )(own, other, seg.reshape(1, ROWS), seg.reshape(ROWS, 1))


def mix_kernel(offset, heads, weights, rows, out, held, sems):
    copies = [
        pltpu.make_async_copy(
            weights.at[:, :, pl.ds((offset + n) * 16, 16), :], held.at[n], sems.at[n]
        )
        for n in range(2)
    ]
    for copy in copies:
        copy.start()
    for n in range(2):
        cols = slice(n * 512, n * 512 + 512)
        copies[n].wait()
        mixed = jnp.dot(heads[...], held[n].reshape(512, 512), preferred_element_type=F32)
        out[:, cols] = (rows[:, cols].astype(F32) + mixed).astype(BF16)


def mix(chunk, heads, w_low, w_high, rows):
    return pl.pallas_call(
        functools.partial(mix_kernel, (2 * chunk) % 4),
        out_shape=jax.ShapeDtypeStruct((ROWS, 1024), BF16),
        in_specs=[VMEM, ANY, VMEM],
        out_specs=VMEM,
        scratch_shapes=[pltpu.VMEM((2, 8, 4, 16, 512), BF16), pltpu.SemaphoreType.DMA((2,))],
        cost_estimate=pl.CostEstimate(
            flops=2 * 128 * 512 * 1024, bytes_accessed=2**20, transcendentals=0
        ),
        name="mix",
    )(heads, w_low if chunk < 2 else w_high, rows)


def per_device(inputs, segment_ids, key_weight, value_weight, out_weight, norm_gain):
    x_part = inputs[0]
    seg = segment_ids[0]
    core_index = lax.axis_index("tensor")
    core = core_index.reshape(1)
    gain = lax.dynamic_slice(norm_gain, (0, core_index * HALF), (1, HALF))
    w_key, w_value, out_low, out_high = gather_weights(
        key_weight[0], value_weight[0], out_weight[0]
    )

    def layer(rows, seg, chunked):
        if chunked:
            before = None
            for chunk in range(CHUNKS):
                last = chunk == CHUNKS - 1
                before = project(core, (chunk,), rows[chunk : chunk + 1], gain, w_key, w_value, before, last)
                if not last:
                    before = before[0]
            own, other = before
        else:
            own, other = project(core, tuple(range(CHUNKS)), rows, gain, w_key, w_value, None, True)
        other = shift(other, "tensor", 1)
        heads = lax.all_gather(attend(own, other, seg), "tensor", axis=1, tiled=True)
        return [mix(chunk, heads, out_low, out_high, rows[chunk]) for chunk in range(CHUNKS)]

    seg_prev = shift(seg, "section", 1)
    seg_prev2 = shift(seg_prev, "section", 1)
    rows = [x_part[:, c * 1024 : c * 1024 + 1024] for c in range(CHUNKS)]
    first = layer(rows, seg, False)
    first = [shift(part, "section", 1) for part in first]
    final = layer(first, seg_prev, True)
    moved = [shift(part, "section", 1) for part in final]
    backup = layer(moved, seg_prev2, True)
    backup = [shift(part, "section", -1) for part in backup]
    return (jnp.concatenate(final, axis=1)[None], jnp.concatenate(backup, axis=1)[None])


def solution(mesh):
    fine = Mesh(mesh.devices.reshape(4, 2, 8, 4), ("section", "tensor", "z", "y"))
    dp = ("z", "y")
    in_specs = (
        P("section", dp, "tensor"),
        P("section", dp),
        P("section", ("tensor",) + dp, None),
        P("section", ("tensor",) + dp, None),
        P("section", dp, "tensor"),
        P("section", None),
    )
    out_specs = (P("section", dp, "tensor"), P("section", dp, "tensor"))
    return jax.shard_map(
        per_device, mesh=fine, in_specs=in_specs, out_specs=out_specs, check_vma=False
    )
```

```python
import functools

import jax
import jax.numpy as jnp
from jax import lax
from jax.experimental import pallas as pl
from jax.experimental.pallas import tpu as pltpu
from jax.sharding import Mesh
from jax.sharding import PartitionSpec as P

D = 8192
HD = 128
ROWS = 128
HALF = 4096
CHUNKS = 4
F32 = jnp.float32
BF16 = jnp.bfloat16
ANY = pl.BlockSpec(memory_space=pl.ANY)
VMEM = pl.BlockSpec(memory_space=pltpu.VMEM)


def shift(block, axis, distance):
    n = lax.axis_size(axis)
    return lax.ppermute(block, axis, [(i, (i + distance) % n) for i in range(n)])


def place(buffer, block, *where):
    start = list(where) + [0] * (buffer.ndim - len(where))
    return lax.dynamic_update_slice(buffer, block, start)


def after(block, *earlier):
    return lax.optimization_barrier((block,) + earlier)[0]


def gather_weights(w_key, w_value, w_out, segs):
    z, y = lax.axis_index("z"), lax.axis_index("y")
    w_out = w_out.reshape(16, 8, 512).transpose(1, 0, 2).reshape(128, 512)
    low = jnp.concatenate([w_key, w_out[:64]], axis=0)
    high = jnp.concatenate([w_value, w_out[64:]], axis=0)

    low_up, low_down = shift(low, "z", 1), shift(low, "z", -1)
    high_up, high_down = shift(high, "y", 1), shift(high, "y", -1)
    low_z = place(place(jnp.zeros((8, 192, 512), BF16), low_up[None], (z + 7) % 8), low_down[None], (z + 1) % 8)
    low_z = place(low_z, low[None], z)
    high_y = place(place(jnp.zeros((4, 192, 512), BF16), high_up[None], (y + 3) % 4), high_down[None], (y + 1) % 4)
    high_y = place(high_y, high[None], y)
    far_up = shift(after(high_up[:96], low_up, low_down, segs[0]), "y", 1)
    far_down = shift(after(high_down[96:], low_up, low_down), "y", -1)
    high_y = place(place(high_y, far_up[None], (y + 2) % 4), far_down[None], (y + 2) % 4, 96)
    up2 = shift(after(low_up, high_down), "z", 1)
    down2 = shift(after(low_down, high_up), "z", -1)
    low_z = place(place(low_z, up2[None], (z + 6) % 8), down2[None], (z + 2) % 8)
    up3 = shift(after(up2, far_up, segs[1]), "z", 1)
    down3 = shift(after(down2, far_down), "z", -1)
    low_z = place(place(low_z, up3[None], (z + 5) % 8), down3[None], (z + 3) % 8)
    high_y = after(high_y, up3, down3)
    up4, down4 = shift(up3[:96], "z", 1), shift(down3[96:], "z", -1)
    low_z = place(place(low_z, up4[None], (z + 4) % 8), down4[None], (z + 4) % 8, 96)

    key = jnp.zeros((8, 4, 128, 512), BF16)
    value = jnp.zeros((8, 4, 128, 512), BF16)
    out_low = jnp.zeros((4, 8, 4, 16, 512), BF16)
    out_high = jnp.zeros((4, 8, 4, 16, 512), BF16)

    def keep_low(buffers, block, first, at):
        key, out = buffers
        many = block.shape[0]
        part = block[:, 128:].reshape(many, 4, 16, 512).transpose(1, 0, 2, 3)
        return (
            place(key, block[:, None, :128], first, at),
            place(out, part[:, :, None], 0, first, at),
        )

    def keep_high(buffers, block, at, first):
        value, out = buffers
        many = block.shape[0]
        part = block[:, 128:].reshape(many, 4, 16, 512).transpose(1, 0, 2, 3)
        return (
            place(value, block[None, :, :128], at, first),
            place(out, part[:, None], 0, at, first),
        )

    lows = keep_low((key, out_low), low_z, 0, y)
    highs = keep_high((value, out_high), high_y, z, 0)
    b_up, b_down = shift(high_y, "z", 1), shift(high_y, "z", -1)
    a_up, a_down = shift(low_z, "y", 1), shift(low_z, "y", -1)
    lows = keep_low(lows, a_up, 0, (y + 3) % 4)
    lows = keep_low(lows, a_down, 0, (y + 1) % 4)
    highs = keep_high(highs, b_up, (z + 7) % 8, 0)
    highs = keep_high(highs, b_down, (z + 1) % 8, 0)
    b_up, b_down = shift(after(b_up, up4), "z", 1), shift(after(b_down, down4), "z", -1)
    highs = keep_high(highs, b_up, (z + 6) % 8, 0)
    highs = keep_high(highs, b_down, (z + 2) % 8, 0)
    b_up, b_down = shift(b_up, "z", 1), shift(b_down, "z", -1)
    highs = keep_high(highs, b_up, (z + 5) % 8, 0)
    highs = keep_high(highs, b_down, (z + 3) % 8, 0)
    lows = keep_low(lows, shift(a_up[:4], "y", 1), 0, (y + 2) % 4)
    lows = keep_low(lows, shift(a_down[4:], "y", -1), 4, (y + 2) % 4)
    highs = keep_high(highs, shift(b_up[:2], "z", 1), (z + 4) % 8, 0)
    highs = keep_high(highs, shift(b_down[2:], "z", -1), (z + 4) % 8, 2)
    return lows[0], highs[0], lows[1].reshape(4, 512, 512), highs[1].reshape(4, 512, 512)


def project_kernel(chunks, first, *refs):
    refs = list(refs)
    rows = [refs.pop(0) for _ in chunks]
    gain, key_hbm, value_hbm = refs.pop(0), refs.pop(0), refs.pop(0)
    before = None if first else refs.pop(0)
    out, key_w, value_w, sems = refs

    copies = []
    for n, chunk in enumerate(chunks):
        part = pl.ds(2 * chunk, 2)
        copies.append(
            (
                pltpu.make_async_copy(key_hbm.at[part], key_w.at[n], sems.at[2 * n]),
                pltpu.make_async_copy(value_hbm.at[part], value_w.at[n], sems.at[2 * n + 1]),
            )
        )
    for pair in copies:
        for copy in pair:
            copy.start()
    if first:
        key_sum = jnp.zeros((ROWS, 512), F32)
        value_sum = jnp.zeros((ROWS, 512), F32)
        squares = jnp.zeros((ROWS, 1), F32)
    else:
        key_sum, value_sum = before[:, :512], before[:, 512:1024]
        squares = before[:, 1024:1025]
    for n, chunk in enumerate(chunks):
        wide = rows[n][...].astype(F32)
        squares = squares + jnp.sum(wide * wide, axis=1, keepdims=True)
        scaled = (wide * gain[:, chunk * 1024 : chunk * 1024 + 1024].astype(F32)).astype(BF16)
        copies[n][0].wait()
        key_sum += jnp.dot(scaled, key_w[n].reshape(1024, 512), preferred_element_type=F32)
        copies[n][1].wait()
        value_sum += jnp.dot(scaled, value_w[n].reshape(1024, 512), preferred_element_type=F32)
    out[:, :512] = key_sum
    out[:, 512:1024] = value_sum
    out[:, 1024:] = jnp.broadcast_to(squares, (ROWS, 128))


def project(chunks, rows, gain, w_key, w_value, before):
    first = before is None
    many = len(chunks)
    return pl.pallas_call(
        functools.partial(project_kernel, chunks, first),
        out_shape=jax.ShapeDtypeStruct((ROWS, 1152), F32),
        in_specs=[VMEM] * many + [VMEM, ANY, ANY] + ([] if first else [VMEM]),
        out_specs=VMEM,
        scratch_shapes=[
            pltpu.VMEM((many, 2, 4, 128, 512), BF16),
            pltpu.VMEM((many, 2, 4, 128, 512), BF16),
            pltpu.SemaphoreType.DMA((2 * many,)),
        ],
        compiler_params=pltpu.CompilerParams(vmem_limit_bytes=(2 * many + 4) * 2**20),
        cost_estimate=pl.CostEstimate(
            flops=many * 2 * 128 * 1024 * 1024, bytes_accessed=many * 2 * 2**20, transcendentals=0
        ),
        name="project",
    )(*rows, gain, w_key, w_value, *([] if first else [before]))


def attend_kernel(own, other_hbm, seg, out, other, sem):
    copy = pltpu.make_async_copy(other_hbm, other, sem)
    copy.start()
    i = lax.broadcasted_iota(jnp.int32, (ROWS, ROWS), 0)
    j = lax.broadcasted_iota(jnp.int32, (ROWS, ROWS), 1)
    wide = jnp.broadcast_to(seg[...].astype(F32), (ROWS, ROWS))
    allowed = (j <= i) & (wide == wide.T)
    copy.wait()
    squares = own[:, 1024:1025] + other[:, 1024:1025]
    scale = lax.rsqrt(squares / D + 1e-05)
    keys = ((own[:, :512] + other[:, :512]) * scale).astype(BF16)
    values = ((own[:, 512:1024] + other[:, 512:1024]) * scale).astype(BF16)
    cols = [slice(head * HD, head * HD + HD) for head in range(4)]
    scores = [
        lax.dot_general(
            keys[:, c], keys[:, c], (((1,), (1,)), ((), ())), preferred_element_type=F32
        )
        / HD
        for c in cols
    ]
    scores = [jnp.where(allowed, each, -1e30) for each in scores]
    lifted = [jnp.exp(each - jnp.max(each, axis=1, keepdims=True)) for each in scores]
    probs = [(each / jnp.sum(each, axis=1, keepdims=True)).astype(BF16) for each in lifted]
    for c, each in zip(cols, probs):
        out[:, c] = jnp.dot(each, values[:, c], preferred_element_type=F32).astype(BF16)


def attend(own, other, seg):
    return pl.pallas_call(
        attend_kernel,
        out_shape=jax.ShapeDtypeStruct((ROWS, 512), BF16),
        in_specs=[VMEM, ANY, VMEM],
        out_specs=VMEM,
        scratch_shapes=[pltpu.VMEM((ROWS, 1152), F32), pltpu.SemaphoreType.DMA],
        compiler_params=pltpu.CompilerParams(vmem_limit_bytes=4 * 2**20),
        name="attend",
    )(own, other, seg)


def mix_kernel(offset, heads, weights, rows, out, held, sems):
    copies = [
        pltpu.make_async_copy(weights.at[offset + n], held.at[n], sems.at[n]) for n in range(2)
    ]
    for copy in copies:
        copy.start()
    for n in range(2):
        cols = slice(n * 512, n * 512 + 512)
        copies[n].wait()
        mixed = jnp.dot(heads[...], held[n], preferred_element_type=F32)
        out[:, cols] = (rows[:, cols].astype(F32) + mixed).astype(BF16)


def mix(chunk, heads, w_low, w_high, rows):
    return pl.pallas_call(
        functools.partial(mix_kernel, (2 * chunk) % 4),
        out_shape=jax.ShapeDtypeStruct((ROWS, 1024), BF16),
        in_specs=[VMEM, ANY, VMEM],
        out_specs=VMEM,
        scratch_shapes=[pltpu.VMEM((2, 512, 512), BF16), pltpu.SemaphoreType.DMA((2,))],
        compiler_params=pltpu.CompilerParams(vmem_limit_bytes=4 * 2**20),
        cost_estimate=pl.CostEstimate(
            flops=2 * 128 * 512 * 1024, bytes_accessed=2**20, transcendentals=0
        ),
        name="mix",
    )(heads, w_low if chunk < 2 else w_high, rows)


def per_device(inputs, segment_ids, key_weight, value_weight, out_weight, norm_gain):
    x_part = inputs[0]
    seg = segment_ids
    core = lax.axis_index("tensor")
    gain = lax.dynamic_slice(norm_gain, (0, core * HALF), (1, HALF))
    seg_prev = shift(seg, "section", 1)
    seg_prev2 = shift(seg_prev, "section", 1)
    w_key, w_value, out_low, out_high = gather_weights(
        key_weight[0], value_weight[0], out_weight[0], (seg_prev, seg_prev2)
    )

    def layer(rows, seg, chunked):
        if chunked:
            own = None
            for chunk in range(CHUNKS):
                own = project((chunk,), rows[chunk : chunk + 1], gain, w_key, w_value, own)
        else:
            own = project(tuple(range(CHUNKS)), rows, gain, w_key, w_value, None)
        heads = attend(own, shift(own, "tensor", 1), seg)
        return [mix(chunk, heads, out_low, out_high, rows[chunk]) for chunk in range(CHUNKS)]

    rows = [x_part[:, c * 1024 : c * 1024 + 1024] for c in range(CHUNKS)]
    first = layer(rows, seg, False)
    first = [shift(part, "section", 1) for part in first]
    final = layer(first, seg_prev, True)
    moved = [shift(part, "section", 1) for part in final]
    backup = layer(moved, seg_prev2, True)
    backup = [shift(part, "section", -1) for part in backup]
    return (jnp.concatenate(final, axis=1)[None], jnp.concatenate(backup, axis=1)[None])


def solution(mesh):
    fine = Mesh(mesh.devices.reshape(4, 2, 8, 4), ("section", "tensor", "z", "y"))
    dp = ("z", "y")
    in_specs = (
        P("section", dp, "tensor"),
        P("section", dp),
        P("section", ("tensor",) + dp, None),
        P("section", ("tensor",) + dp, None),
        P("section", dp, "tensor"),
        P("section", None),
    )
    out_specs = (P("section", dp, "tensor"), P("section", dp, "tensor"))
    return jax.shard_map(
        per_device, mesh=fine, in_specs=in_specs, out_specs=out_specs, check_vma=False
    )
```

```python
import functools

import jax
import jax.numpy as jnp
from jax import lax
from jax.experimental import pallas as pl
from jax.experimental.pallas import tpu as pltpu
from jax.sharding import Mesh
from jax.sharding import PartitionSpec as P

D = 8192
HD = 128
ROWS = 128
HALF = 4096
CHUNKS = 2
WIDTH = HALF // CHUNKS
DEPTH = 8 // CHUNKS
F32 = jnp.float32
BF16 = jnp.bfloat16
ANY = pl.BlockSpec(memory_space=pl.ANY)
VMEM = pl.BlockSpec(memory_space=pltpu.VMEM)


def shift(block, axis, distance):
    n = lax.axis_size(axis)
    return lax.ppermute(block, axis, [(i, (i + distance) % n) for i in range(n)])


def place(buffer, block, *where):
    start = list(where) + [0] * (buffer.ndim - len(where))
    return lax.dynamic_update_slice(buffer, block, start)


def after(block, *earlier):
    return lax.optimization_barrier((block,) + earlier)[0]


def blocks_of(w_out):
    return w_out.reshape(16, 8, 512).transpose(1, 0, 2).reshape(128, 512)


def gather_weights(w_key, w_value, w_out, w_late, seg):
    z, y = lax.axis_index("z"), lax.axis_index("y")
    w_out = blocks_of(w_out)
    low = jnp.concatenate([w_key, w_out[:64]], axis=0)
    high = jnp.concatenate([w_value, w_out[64:], w_late], axis=0)

    low_up, low_down = shift(low, "z", 1), shift(low, "z", -1)
    high_up, high_down = shift(high, "y", 1), shift(high, "y", -1)
    low_z = place(place(jnp.zeros((8, 192, 512), BF16), low_up[None], (z + 7) % 8), low_down[None], (z + 1) % 8)
    low_z = place(low_z, low[None], z)
    high_y = place(place(jnp.zeros((4, 320, 512), BF16), high_up[None], (y + 3) % 4), high_down[None], (y + 1) % 4)
    high_y = place(high_y, high[None], y)
    far_up = shift(after(high_up[:160], low_up, low_down), "y", 1)
    far_down = shift(after(high_down[160:], low_up, low_down), "y", -1)
    high_y = place(place(high_y, far_up[None], (y + 2) % 4), far_down[None], (y + 2) % 4, 160)
    up2 = shift(low_up, "z", 1)
    down2 = shift(low_down, "z", -1)
    low_z = place(place(low_z, up2[None], (z + 6) % 8), down2[None], (z + 2) % 8)
    up3 = shift(after(up2, far_up), "z", 1)
    down3 = shift(after(down2, far_down), "z", -1)
    low_z = place(place(low_z, up3[None], (z + 5) % 8), down3[None], (z + 3) % 8)
    late_y = high_y[:, 192:]
    high_y = after(high_y[:, :192], up3, down3)
    up4, down4 = shift(up3[:96], "z", 1), shift(down3[96:], "z", -1)
    low_z = place(place(low_z, up4[None], (z + 4) % 8), down4[None], (z + 4) % 8, 96)

    key = jnp.zeros((8, 4, 128, 512), BF16)
    value = jnp.zeros((8, 4, 128, 512), BF16)
    out_low = jnp.zeros((4, 8, 4, 16, 512), BF16)
    out_high = jnp.zeros((4, 8, 4, 16, 512), BF16)

    def keep_low(buffers, block, first, at):
        key, out = buffers
        many = block.shape[0]
        part = block[:, 128:].reshape(many, 4, 16, 512).transpose(1, 0, 2, 3)
        return (
            place(key, block[:, None, :128], first, at),
            place(out, part[:, :, None], 0, first, at),
        )

    def keep_high(buffers, block, at, first):
        value, out = buffers
        many = block.shape[0]
        part = block[:, 128:].reshape(many, 4, 16, 512).transpose(1, 0, 2, 3)
        return (
            place(value, block[None, :, :128], at, first),
            place(out, part[:, None], 0, at, first),
        )

    lows = keep_low((key, out_low), low_z, 0, y)
    highs = keep_high((value, out_high), high_y, z, 0)
    b_up, b_down = shift(high_y, "z", 1), shift(high_y, "z", -1)
    a_up, a_down = shift(low_z, "y", 1), shift(low_z, "y", -1)
    lows = keep_low(lows, a_up, 0, (y + 3) % 4)
    lows = keep_low(lows, a_down, 0, (y + 1) % 4)
    seg = after(seg, b_up, b_down)
    segs = shift(seg, "section", 1), shift(seg, "section", 2)
    highs = keep_high(highs, b_up, (z + 7) % 8, 0)
    highs = keep_high(highs, b_down, (z + 1) % 8, 0)
    b_up, b_down = shift(after(b_up, up4), "z", 1), shift(after(b_down, down4), "z", -1)
    highs = keep_high(highs, b_up, (z + 6) % 8, 0)
    highs = keep_high(highs, b_down, (z + 2) % 8, 0)
    b_up, b_down = shift(b_up, "z", 1), shift(b_down, "z", -1)
    highs = keep_high(highs, b_up, (z + 5) % 8, 0)
    highs = keep_high(highs, b_down, (z + 3) % 8, 0)
    lows = keep_low(lows, shift(a_up[:4], "y", 1), 0, (y + 2) % 4)
    lows = keep_low(lows, shift(a_down[4:], "y", -1), 4, (y + 2) % 4)
    b_up, b_down = shift(b_up[:2], "z", 1), shift(b_down[2:], "z", -1)
    highs = keep_high(highs, b_up, (z + 4) % 8, 0)
    highs = keep_high(highs, b_down, (z + 4) % 8, 2)
    late_y = after(late_y, b_up, b_down)
    lows, highs = (lows[0], lows[1].reshape(4, 512, 512)), (highs[0], highs[1].reshape(4, 512, 512))
    return lows[0], highs[0], lows[1], highs[1], late_y, segs


def project_kernel(chunks, first, *refs):
    refs = list(refs)
    rows = [refs.pop(0) for _ in chunks]
    gain, key_hbm, value_hbm = refs.pop(0), refs.pop(0), refs.pop(0)
    before = None if first else refs.pop(0)
    out, key_w, value_w, sems = refs

    copies = []
    for n, chunk in enumerate(chunks):
        part = pl.ds(DEPTH * chunk, DEPTH)
        copies.append(
            (
                pltpu.make_async_copy(key_hbm.at[part], key_w.at[n], sems.at[2 * n]),
                pltpu.make_async_copy(value_hbm.at[part], value_w.at[n], sems.at[2 * n + 1]),
            )
        )
    for pair in copies:
        for copy in pair:
            copy.start()
    if first:
        key_sum = jnp.zeros((ROWS, 512), F32)
        value_sum = jnp.zeros((ROWS, 512), F32)
        squares = jnp.zeros((ROWS, 1), F32)
    else:
        key_sum, value_sum = before[:, :512], before[:, 512:1024]
        squares = before[:, 1024:1025]
    for n, chunk in enumerate(chunks):
        wide = rows[n][...].astype(F32)
        squares = squares + jnp.sum(wide * wide, axis=1, keepdims=True)
        scaled = (wide * gain[:, chunk * WIDTH : chunk * WIDTH + WIDTH].astype(F32)).astype(BF16)
        copies[n][0].wait()
        key_sum += jnp.dot(scaled, key_w[n].reshape(WIDTH, 512), preferred_element_type=F32)
        copies[n][1].wait()
        value_sum += jnp.dot(scaled, value_w[n].reshape(WIDTH, 512), preferred_element_type=F32)
    out[:, :512] = key_sum
    out[:, 512:1024] = value_sum
    out[:, 1024:] = jnp.broadcast_to(squares, (ROWS, 128))


def project(chunks, rows, gain, w_key, w_value, before):
    first = before is None
    many = len(chunks)
    return pl.pallas_call(
        functools.partial(project_kernel, chunks, first),
        out_shape=jax.ShapeDtypeStruct((ROWS, 1152), F32),
        in_specs=[VMEM] * many + [VMEM, ANY, ANY] + ([] if first else [VMEM]),
        out_specs=VMEM,
        scratch_shapes=[
            pltpu.VMEM((many, DEPTH, 4, 128, 512), BF16),
            pltpu.VMEM((many, DEPTH, 4, 128, 512), BF16),
            pltpu.SemaphoreType.DMA((2 * many,)),
        ],
        compiler_params=pltpu.CompilerParams(vmem_limit_bytes=(many * DEPTH + 8) * 2**20),
        cost_estimate=pl.CostEstimate(
            flops=many * 2 * 128 * WIDTH * 1024, bytes_accessed=many * WIDTH * 2048, transcendentals=0
        ),
        name="project",
    )(*rows, gain, w_key, w_value, *([] if first else [before]))


def attend_kernel(own, other_hbm, seg, out, other, sem):
    copy = pltpu.make_async_copy(other_hbm, other, sem)
    copy.start()
    i = lax.broadcasted_iota(jnp.int32, (ROWS, ROWS), 0)
    j = lax.broadcasted_iota(jnp.int32, (ROWS, ROWS), 1)
    wide = jnp.broadcast_to(seg[...].astype(F32), (ROWS, ROWS))
    allowed = (j <= i) & (wide == wide.T)
    copy.wait()
    squares = own[:, 1024:1025] + other[:, 1024:1025]
    scale = lax.rsqrt(squares / D + 1e-05)
    keys = ((own[:, :512] + other[:, :512]) * scale).astype(BF16)
    values = ((own[:, 512:1024] + other[:, 512:1024]) * scale).astype(BF16)
    cols = [slice(head * HD, head * HD + HD) for head in range(4)]
    scores = [
        lax.dot_general(
            keys[:, c], keys[:, c], (((1,), (1,)), ((), ())), preferred_element_type=F32
        )
        / HD
        for c in cols
    ]
    scores = [jnp.where(allowed, each, -1e30) for each in scores]
    lifted = [jnp.exp(each - jnp.max(each, axis=1, keepdims=True)) for each in scores]
    probs = [(each / jnp.sum(each, axis=1, keepdims=True)).astype(BF16) for each in lifted]
    for c, each in zip(cols, probs):
        out[:, c] = jnp.dot(each, values[:, c], preferred_element_type=F32).astype(BF16)


def attend(own, other, seg):
    return pl.pallas_call(
        attend_kernel,
        out_shape=jax.ShapeDtypeStruct((ROWS, 512), BF16),
        in_specs=[VMEM, ANY, VMEM],
        out_specs=VMEM,
        scratch_shapes=[pltpu.VMEM((ROWS, 1152), F32), pltpu.SemaphoreType.DMA],
        compiler_params=pltpu.CompilerParams(vmem_limit_bytes=4 * 2**20),
        name="attend",
    )(own, other, seg)


def mix_kernel(places, *refs):
    sources = refs[: 1 + max(which for which, _ in places)]
    heads, rows, out, held, sems = refs[len(sources) :]
    copies = [
        pltpu.make_async_copy(sources[which].at[index], held.at[n], sems.at[n])
        for n, (which, index) in enumerate(places)
    ]
    for copy in copies:
        copy.start()
    for n, copy in enumerate(copies):
        cols = slice(n * 512, n * 512 + 512)
        copy.wait()
        mixed = jnp.dot(heads[...], held[n], preferred_element_type=F32)
        out[:, cols] = (rows[:, cols].astype(F32) + mixed).astype(BF16)


def mix(weights, heads, rows):
    sources = []
    places = []
    for array, index in weights:
        found = [n for n, other in enumerate(sources) if other is array]
        if not found:
            sources.append(array)
        places.append((found[0] if found else len(sources) - 1, index))
    many = len(places)
    return pl.pallas_call(
        functools.partial(mix_kernel, tuple(places)),
        out_shape=jax.ShapeDtypeStruct((ROWS, many * 512), BF16),
        in_specs=[ANY] * len(sources) + [VMEM, VMEM],
        out_specs=VMEM,
        scratch_shapes=[pltpu.VMEM((many, 512, 512), BF16), pltpu.SemaphoreType.DMA((many,))],
        compiler_params=pltpu.CompilerParams(vmem_limit_bytes=(many // 2 + 5) * 2**20),
        cost_estimate=pl.CostEstimate(
            flops=2 * 128 * 512 * 512 * many, bytes_accessed=many * 2**19, transcendentals=0
        ),
        name="mix",
    )(*sources, heads, rows)


class Late:
    def __init__(self, own):
        z = lax.axis_index("z")
        self.z, self.up, self.down, self.step = z, own, own, 0
        self.held = jnp.zeros((8, 8, 4, 16, 512), BF16)
        self.keep(own, 0, 0)

    def keep(self, block, offset, first):
        part = block.reshape(block.shape[0], 8, 16, 512).transpose(1, 0, 2, 3)
        self.held = place(self.held, part[:, None], 0, (self.z + offset) % 8, first)

    def advance(self, *earlier):
        self.step += 1
        up, down = after(self.up, *earlier), after(self.down, *earlier)
        if self.step < 4:
            self.up, self.down = shift(up, "z", 1), shift(down, "z", -1)
            self.keep(self.up, 8 - self.step, 0)
            self.keep(self.down, self.step, 0)
        else:
            self.keep(shift(up[:2], "z", 1), 4, 0)
            self.keep(shift(down[2:], "z", -1), 4, 2)

    def blocks(self):
        return self.held.reshape(8, 512, 512)


def per_device(inputs, segment_ids, key_weight, value_weight, out_weight, norm_gain):
    x_part = inputs[0]
    core = lax.axis_index("tensor")
    gain = lax.dynamic_slice(norm_gain, (0, core * HALF), (1, HALF))
    w_next = blocks_of(shift(out_weight[0], "section", -1))
    seg = segment_ids
    w_key, w_value, out_low, out_high, late_y, (seg_prev, seg_prev2) = gather_weights(
        key_weight[0], value_weight[0], out_weight[0], w_next, seg
    )
    late = Late(late_y)
    own = [(out_low, n) if n < 4 else (out_high, n - 4) for n in range(8)]
    parts = range(CHUNKS)
    many = 8 // CHUNKS

    def heads_of(sums, seg):
        return attend(sums, shift(sums, "tensor", 1), seg)

    def mixed(heads, rows):
        return [mix(own[c * many : c * many + many], heads, rows[c]) for c in parts]

    def projected(rows):
        sums = None
        for c in parts:
            sums = project((c,), rows[c : c + 1], gain, w_key, w_value, sums)
        return sums

    rows = [x_part[:, c * WIDTH : c * WIDTH + WIDTH] for c in parts]
    heads = heads_of(project(tuple(parts), rows, gain, w_key, w_value, None), seg)
    first = mixed(heads, rows)
    late.advance()
    late.advance(*first)
    late.advance()
    first = [shift(part, "section", 1) for part in first]
    heads = heads_of(projected(first), seg_prev)
    final = mixed(heads, first)
    late.advance(*final)
    moved = [shift(part, "section", 1) for part in final]
    heads = heads_of(projected(moved), seg_prev2)
    heads = shift(heads, "section", -1)
    final = jnp.concatenate(final, axis=1)
    following = late.blocks()
    backup = mix([(following, n) for n in range(8)], heads, final)
    return (final[None], backup[None])


def solution(mesh):
    fine = Mesh(mesh.devices.reshape(4, 2, 8, 4), ("section", "tensor", "z", "y"))
    dp = ("z", "y")
    in_specs = (
        P("section", dp, "tensor"),
        P("section", dp),
        P("section", ("tensor",) + dp, None),
        P("section", ("tensor",) + dp, None),
        P("section", dp, "tensor"),
        P("section", None),
    )
    out_specs = (P("section", dp, "tensor"), P("section", dp, "tensor"))
    return jax.shard_map(
        per_device, mesh=fine, in_specs=in_specs, out_specs=out_specs, check_vma=False
    )
```

```python
import functools

import jax
import jax.numpy as jnp
from jax import lax
from jax.experimental import pallas as pl
from jax.experimental.pallas import tpu as pltpu
from jax.sharding import Mesh
from jax.sharding import PartitionSpec as P

D = 8192
HD = 128
ROWS = 128
HALF = 4096
CHUNKS = 2
WIDTH = HALF // CHUNKS
DEPTH = 8 // CHUNKS
LOW = 5
F32 = jnp.float32
BF16 = jnp.bfloat16
ANY = pl.BlockSpec(memory_space=pl.ANY)
VMEM = pl.BlockSpec(memory_space=pltpu.VMEM)


def shift(block, axis, distance):
    n = lax.axis_size(axis)
    return lax.ppermute(block, axis, [(i, (i + distance) % n) for i in range(n)])


def place(buffer, block, *where):
    start = list(where) + [0] * (buffer.ndim - len(where))
    return lax.dynamic_update_slice(buffer, block, start)


def after(block, *earlier):
    return lax.optimization_barrier((block,) + earlier)[0]


def blocks_of(w_out):
    return w_out.reshape(16, 8, 512).transpose(1, 0, 2).reshape(128, 512)


def gather_weights(w_key, w_value, w_out, w_late, seg):
    z, y = lax.axis_index("z"), lax.axis_index("y")
    w_out = blocks_of(w_out)
    low = jnp.concatenate([w_key, w_out[: LOW * 16]], axis=0)
    high = jnp.concatenate([w_value, w_out[LOW * 16 :], w_late], axis=0)
    n_low, n_high, n_soon = 128 + LOW * 16, 384 - LOW * 16, 256 - LOW * 16
    h_low, h_high = n_low // 2, n_high // 2

    low_up, low_down = shift(low, "z", 1), shift(low, "z", -1)
    high = after(high, low_up, low_down)
    high_up, high_down = shift(high, "y", 1), shift(high, "y", -1)
    low_z = place(place(jnp.zeros((8, n_low, 512), BF16), low_up[None], (z + 7) % 8), low_down[None], (z + 1) % 8)
    low_z = place(low_z, low[None], z)
    high_y = place(place(jnp.zeros((4, n_high, 512), BF16), high_up[None], (y + 3) % 4), high_down[None], (y + 1) % 4)
    high_y = place(high_y, high[None], y)
    up2 = shift(low_up, "z", 1)
    down2 = shift(low_down, "z", -1)
    low_z = place(place(low_z, up2[None], (z + 6) % 8), down2[None], (z + 2) % 8)
    far_up = shift(after(high_up[:h_high], up2, down2), "y", 1)
    far_down = shift(after(high_down[h_high:], up2, down2), "y", -1)
    high_y = place(place(high_y, far_up[None], (y + 2) % 4), far_down[None], (y + 2) % 4, h_high)
    up3 = shift(up2, "z", 1)
    down3 = shift(down2, "z", -1)
    low_z = place(place(low_z, up3[None], (z + 5) % 8), down3[None], (z + 3) % 8)
    late_y = high_y[:, n_soon:]
    high_y = after(high_y[:, :n_soon], up3, down3)
    up4, down4 = shift(up3[:h_low], "z", 1), shift(down3[h_low:], "z", -1)
    low_z = place(place(low_z, up4[None], (z + 4) % 8), down4[None], (z + 4) % 8, h_low)

    key = jnp.zeros((8, 4, 128, 512), BF16)
    value = jnp.zeros((8, 4, 128, 512), BF16)
    out_low = jnp.zeros((LOW, 8, 4, 16, 512), BF16)
    out_high = jnp.zeros((8 - LOW, 8, 4, 16, 512), BF16)

    def keep_low(buffers, block, first, at):
        key, out = buffers
        many = block.shape[0]
        part = block[:, 128:].reshape(many, -1, 16, 512).transpose(1, 0, 2, 3)
        return (
            place(key, block[:, None, :128], first, at),
            place(out, part[:, :, None], 0, first, at),
        )

    def keep_high(buffers, block, at, first):
        value, out = buffers
        many = block.shape[0]
        part = block[:, 128:].reshape(many, -1, 16, 512).transpose(1, 0, 2, 3)
        return (
            place(value, block[None, :, :128], at, first),
            place(out, part[:, None], 0, at, first),
        )

    lows = keep_low((key, out_low), low_z, 0, y)
    highs = keep_high((value, out_high), high_y, z, 0)
    b_up, b_down = shift(high_y, "z", 1), shift(high_y, "z", -1)
    a_up, a_down = shift(low_z, "y", 1), shift(low_z, "y", -1)
    lows = keep_low(lows, a_up, 0, (y + 3) % 4)
    lows = keep_low(lows, a_down, 0, (y + 1) % 4)
    seg = after(seg, b_up, b_down)
    segs = shift(seg, "section", 1), shift(seg, "section", 2)
    highs = keep_high(highs, b_up, (z + 7) % 8, 0)
    highs = keep_high(highs, b_down, (z + 1) % 8, 0)
    b_up, b_down = shift(after(b_up, up4), "z", 1), shift(after(b_down, down4), "z", -1)
    highs = keep_high(highs, b_up, (z + 6) % 8, 0)
    highs = keep_high(highs, b_down, (z + 2) % 8, 0)
    b_up, b_down = shift(b_up, "z", 1), shift(b_down, "z", -1)
    highs = keep_high(highs, b_up, (z + 5) % 8, 0)
    highs = keep_high(highs, b_down, (z + 3) % 8, 0)
    lows = keep_low(lows, shift(a_up[:4], "y", 1), 0, (y + 2) % 4)
    lows = keep_low(lows, shift(a_down[4:], "y", -1), 4, (y + 2) % 4)
    b_up, b_down = shift(b_up[:2], "z", 1), shift(b_down[2:], "z", -1)
    highs = keep_high(highs, b_up, (z + 4) % 8, 0)
    highs = keep_high(highs, b_down, (z + 4) % 8, 2)
    late_y = after(late_y, b_up, b_down)
    lows, highs = (lows[0], lows[1].reshape(-1, 512, 512)), (highs[0], highs[1].reshape(-1, 512, 512))
    return lows[0], highs[0], lows[1], highs[1], late_y, segs


def project_kernel(chunks, first, *refs):
    refs = list(refs)
    rows = [refs.pop(0) for _ in chunks]
    gain, key_hbm, value_hbm = refs.pop(0), refs.pop(0), refs.pop(0)
    before = None if first else refs.pop(0)
    out, key_w, value_w, sems = refs

    copies = []
    for n, chunk in enumerate(chunks):
        part = pl.ds(DEPTH * chunk, DEPTH)
        copies.append(
            (
                pltpu.make_async_copy(key_hbm.at[part], key_w.at[n], sems.at[2 * n]),
                pltpu.make_async_copy(value_hbm.at[part], value_w.at[n], sems.at[2 * n + 1]),
            )
        )
    for pair in copies:
        for copy in pair:
            copy.start()
    if first:
        key_sum = jnp.zeros((ROWS, 512), F32)
        value_sum = jnp.zeros((ROWS, 512), F32)
        squares = jnp.zeros((ROWS, 1), F32)
    else:
        key_sum, value_sum = before[:, :512], before[:, 512:1024]
        squares = before[:, 1024:1025]
    for n, chunk in enumerate(chunks):
        wide = rows[n][...].astype(F32)
        squares = squares + jnp.sum(wide * wide, axis=1, keepdims=True)
        scaled = (wide * gain[:, chunk * WIDTH : chunk * WIDTH + WIDTH].astype(F32)).astype(BF16)
        copies[n][0].wait()
        key_sum += jnp.dot(scaled, key_w[n].reshape(WIDTH, 512), preferred_element_type=F32)
        copies[n][1].wait()
        value_sum += jnp.dot(scaled, value_w[n].reshape(WIDTH, 512), preferred_element_type=F32)
    out[:, :512] = key_sum
    out[:, 512:1024] = value_sum
    out[:, 1024:] = jnp.broadcast_to(squares, (ROWS, 128))


def project(chunks, rows, gain, w_key, w_value, before):
    first = before is None
    many = len(chunks)
    return pl.pallas_call(
        functools.partial(project_kernel, chunks, first),
        out_shape=jax.ShapeDtypeStruct((ROWS, 1152), F32),
        in_specs=[VMEM] * many + [VMEM, ANY, ANY] + ([] if first else [VMEM]),
        out_specs=VMEM,
        scratch_shapes=[
            pltpu.VMEM((many, DEPTH, 4, 128, 512), BF16),
            pltpu.VMEM((many, DEPTH, 4, 128, 512), BF16),
            pltpu.SemaphoreType.DMA((2 * many,)),
        ],
        compiler_params=pltpu.CompilerParams(vmem_limit_bytes=(many * DEPTH + 8) * 2**20),
        cost_estimate=pl.CostEstimate(
            flops=many * 2 * 128 * WIDTH * 1024, bytes_accessed=many * WIDTH * 2048, transcendentals=0
        ),
        name="project",
    )(*rows, gain, w_key, w_value, *([] if first else [before]))


def attend_kernel(own, other_hbm, seg, out, other, sem):
    copy = pltpu.make_async_copy(other_hbm, other, sem)
    copy.start()
    i = lax.broadcasted_iota(jnp.int32, (ROWS, ROWS), 0)
    j = lax.broadcasted_iota(jnp.int32, (ROWS, ROWS), 1)
    wide = jnp.broadcast_to(seg[...].astype(F32), (ROWS, ROWS))
    allowed = (j <= i) & (wide == wide.T)
    copy.wait()
    squares = own[:, 1024:1025] + other[:, 1024:1025]
    scale = lax.rsqrt(squares / D + 1e-05)
    keys = ((own[:, :512] + other[:, :512]) * scale).astype(BF16)
    values = ((own[:, 512:1024] + other[:, 512:1024]) * scale).astype(BF16)
    cols = [slice(head * HD, head * HD + HD) for head in range(4)]
    scores = [
        lax.dot_general(
            keys[:, c], keys[:, c], (((1,), (1,)), ((), ())), preferred_element_type=F32
        )
        / HD
        for c in cols
    ]
    scores = [jnp.where(allowed, each, -1e30) for each in scores]
    lifted = [jnp.exp(each - jnp.max(each, axis=1, keepdims=True)) for each in scores]
    probs = [(each / jnp.sum(each, axis=1, keepdims=True)).astype(BF16) for each in lifted]
    for c, each in zip(cols, probs):
        out[:, c] = jnp.dot(each, values[:, c], preferred_element_type=F32).astype(BF16)


def attend(own, other, seg):
    return pl.pallas_call(
        attend_kernel,
        out_shape=jax.ShapeDtypeStruct((ROWS, 512), BF16),
        in_specs=[VMEM, ANY, VMEM],
        out_specs=VMEM,
        scratch_shapes=[pltpu.VMEM((ROWS, 1152), F32), pltpu.SemaphoreType.DMA],
        compiler_params=pltpu.CompilerParams(vmem_limit_bytes=4 * 2**20),
        name="attend",
    )(own, other, seg)


def mix_kernel(places, *refs):
    sources = refs[: 1 + max(which for which, _ in places)]
    heads, rows, out, held, sems = refs[len(sources) :]
    copies = [
        pltpu.make_async_copy(sources[which].at[index], held.at[n], sems.at[n])
        for n, (which, index) in enumerate(places)
    ]
    for copy in copies:
        copy.start()
    for n, copy in enumerate(copies):
        cols = slice(n * 512, n * 512 + 512)
        copy.wait()
        mixed = jnp.dot(heads[...], held[n], preferred_element_type=F32)
        out[:, cols] = (rows[:, cols].astype(F32) + mixed).astype(BF16)


def mix(weights, heads, rows):
    sources = []
    places = []
    for array, index in weights:
        found = [n for n, other in enumerate(sources) if other is array]
        if not found:
            sources.append(array)
        places.append((found[0] if found else len(sources) - 1, index))
    many = len(places)
    return pl.pallas_call(
        functools.partial(mix_kernel, tuple(places)),
        out_shape=jax.ShapeDtypeStruct((ROWS, many * 512), BF16),
        in_specs=[ANY] * len(sources) + [VMEM, VMEM],
        out_specs=VMEM,
        scratch_shapes=[pltpu.VMEM((many, 512, 512), BF16), pltpu.SemaphoreType.DMA((many,))],
        compiler_params=pltpu.CompilerParams(vmem_limit_bytes=(many // 2 + 5) * 2**20),
        cost_estimate=pl.CostEstimate(
            flops=2 * 128 * 512 * 512 * many, bytes_accessed=many * 2**19, transcendentals=0
        ),
        name="mix",
    )(*sources, heads, rows)


class Late:
    def __init__(self, own):
        z = lax.axis_index("z")
        self.z, self.up, self.down, self.step = z, own, own, 0
        self.held = jnp.zeros((8, 8, 4, 16, 512), BF16)
        self.keep(own, 0, 0)

    def keep(self, block, offset, first):
        part = block.reshape(block.shape[0], 8, 16, 512).transpose(1, 0, 2, 3)
        self.held = place(self.held, part[:, None], 0, (self.z + offset) % 8, first)

    def advance(self, *earlier):
        self.step += 1
        up, down = after(self.up, *earlier), after(self.down, *earlier)
        if self.step < 4:
            self.up, self.down = shift(up, "z", 1), shift(down, "z", -1)
            self.keep(self.up, 8 - self.step, 0)
            self.keep(self.down, self.step, 0)
        else:
            self.keep(shift(up[:2], "z", 1), 4, 0)
            self.keep(shift(down[2:], "z", -1), 4, 2)

    def blocks(self):
        return self.held.reshape(8, 512, 512)


def per_device(inputs, segment_ids, key_weight, value_weight, out_weight, norm_gain):
    x_part = inputs[0]
    core = lax.axis_index("tensor")
    gain = lax.dynamic_slice(norm_gain, (0, core * HALF), (1, HALF))
    w_next = blocks_of(shift(out_weight[0], "section", -1))
    seg = segment_ids
    w_key, w_value, out_low, out_high, late_y, (seg_prev, seg_prev2) = gather_weights(
        key_weight[0], value_weight[0], out_weight[0], w_next, seg
    )
    late = Late(late_y)
    own = [(out_low, n) if n < LOW else (out_high, n - LOW) for n in range(8)]
    parts = range(CHUNKS)
    many = 8 // CHUNKS

    def heads_of(sums, seg):
        return attend(sums, shift(sums, "tensor", 1), seg)

    def mixed(heads, rows):
        return [mix(own[c * many : c * many + many], heads, rows[c]) for c in parts]

    def projected(rows):
        sums = None
        for c in parts:
            sums = project((c,), rows[c : c + 1], gain, w_key, w_value, sums)
        return sums

    rows = [x_part[:, c * WIDTH : c * WIDTH + WIDTH] for c in parts]
    heads = heads_of(project(tuple(parts), rows, gain, w_key, w_value, None), seg)
    first = mixed(heads, rows)
    late.advance()
    late.advance(*first)
    late.advance()
    first = [shift(part, "section", 1) for part in first]
    heads = heads_of(projected(first), seg_prev)
    final = mixed(heads, first)
    late.advance(*final)
    moved = [shift(part, "section", 1) for part in final]
    heads = heads_of(projected(moved), seg_prev2)
    heads = shift(heads, "section", -1)
    final = jnp.concatenate(final, axis=1)
    following = late.blocks()
    backup = mix([(following, n) for n in range(8)], heads, final)
    return (final[None], backup[None])


def solution(mesh):
    fine = Mesh(mesh.devices.reshape(4, 2, 8, 4), ("section", "tensor", "z", "y"))
    dp = ("z", "y")
    in_specs = (
        P("section", dp, "tensor"),
        P("section", dp),
        P("section", ("tensor",) + dp, None),
        P("section", ("tensor",) + dp, None),
        P("section", dp, "tensor"),
        P("section", None),
    )
    out_specs = (P("section", dp, "tensor"), P("section", dp, "tensor"))
    return jax.shard_map(
        per_device, mesh=fine, in_specs=in_specs, out_specs=out_specs, check_vma=False
    )
```

```python
import functools

import jax
import jax.numpy as jnp
from jax import lax
from jax.experimental import pallas as pl
from jax.experimental.pallas import tpu as pltpu
from jax.sharding import Mesh
from jax.sharding import PartitionSpec as P

D = 8192
HD = 128
ROWS = 128
HALF = 4096
CHUNKS = 4
WIDTH = HALF // CHUNKS
DEPTH = 8 // CHUNKS
LOW = 5
F32 = jnp.float32
BF16 = jnp.bfloat16
ANY = pl.BlockSpec(memory_space=pl.ANY)
VMEM = pl.BlockSpec(memory_space=pltpu.VMEM)


def shift(block, axis, distance):
    n = lax.axis_size(axis)
    return lax.ppermute(block, axis, [(i, (i + distance) % n) for i in range(n)])


def place(buffer, block, *where):
    start = list(where) + [0] * (buffer.ndim - len(where))
    return lax.dynamic_update_slice(buffer, block, start)


def after(block, *earlier):
    return lax.optimization_barrier((block,) + earlier)[0]


def blocks_of(w_out):
    return w_out.reshape(16, 8, 512).transpose(1, 0, 2).reshape(128, 512)


def gather_weights(w_key, w_value, w_out, w_late, seg):
    z, y = lax.axis_index("z"), lax.axis_index("y")
    w_out = blocks_of(w_out)
    low = jnp.concatenate([w_key, w_out[: LOW * 16]], axis=0)
    high = jnp.concatenate([w_value, w_out[LOW * 16 :], w_late], axis=0)
    n_low, n_high, n_soon = 128 + LOW * 16, 384 - LOW * 16, 256 - LOW * 16
    h_low, h_high = n_low // 2, n_high // 2

    low_up, low_down = shift(low, "z", 1), shift(low, "z", -1)
    high = after(high, low_up, low_down)
    high_up, high_down = shift(high, "y", 1), shift(high, "y", -1)
    low_z = place(place(jnp.zeros((8, n_low, 512), BF16), low_up[None], (z + 7) % 8), low_down[None], (z + 1) % 8)
    low_z = place(low_z, low[None], z)
    high_y = place(place(jnp.zeros((4, n_high, 512), BF16), high_up[None], (y + 3) % 4), high_down[None], (y + 1) % 4)
    high_y = place(high_y, high[None], y)
    up2 = shift(low_up, "z", 1)
    down2 = shift(low_down, "z", -1)
    low_z = place(place(low_z, up2[None], (z + 6) % 8), down2[None], (z + 2) % 8)
    far_up = shift(after(high_up[:h_high], up2, down2), "y", 1)
    far_down = shift(after(high_down[h_high:], up2, down2), "y", -1)
    high_y = place(place(high_y, far_up[None], (y + 2) % 4), far_down[None], (y + 2) % 4, h_high)
    up3 = shift(up2, "z", 1)
    down3 = shift(down2, "z", -1)
    low_z = place(place(low_z, up3[None], (z + 5) % 8), down3[None], (z + 3) % 8)
    late_y = high_y[:, n_soon:]
    high_y = after(high_y[:, :n_soon], up3, down3)
    up4, down4 = shift(up3[:h_low], "z", 1), shift(down3[h_low:], "z", -1)
    low_z = place(place(low_z, up4[None], (z + 4) % 8), down4[None], (z + 4) % 8, h_low)

    key = jnp.zeros((8, 4, 128, 512), BF16)
    value = jnp.zeros((8, 4, 128, 512), BF16)
    out_low = jnp.zeros((LOW, 8, 4, 16, 512), BF16)
    out_high = jnp.zeros((8 - LOW, 8, 4, 16, 512), BF16)

    def keep_low(buffers, block, first, at):
        key, out = buffers
        many = block.shape[0]
        part = block[:, 128:].reshape(many, -1, 16, 512).transpose(1, 0, 2, 3)
        return (
            place(key, block[:, None, :128], first, at),
            place(out, part[:, :, None], 0, first, at),
        )

    def keep_high(buffers, block, at, first):
        value, out = buffers
        many = block.shape[0]
        part = block[:, 128:].reshape(many, -1, 16, 512).transpose(1, 0, 2, 3)
        return (
            place(value, block[None, :, :128], at, first),
            place(out, part[:, None], 0, at, first),
        )

    lows = keep_low((key, out_low), low_z, 0, y)
    highs = keep_high((value, out_high), high_y, z, 0)
    b_up, b_down = shift(high_y, "z", 1), shift(high_y, "z", -1)
    a_up, a_down = shift(low_z, "y", 1), shift(low_z, "y", -1)
    lows = keep_low(lows, a_up, 0, (y + 3) % 4)
    lows = keep_low(lows, a_down, 0, (y + 1) % 4)
    prev = shift(after(seg, b_up, b_down), "section", 1)
    highs = keep_high(highs, b_up, (z + 7) % 8, 0)
    highs = keep_high(highs, b_down, (z + 1) % 8, 0)
    b_up, b_down = shift(after(b_up, up4), "z", 1), shift(after(b_down, down4), "z", -1)
    segs = prev, shift(after(seg, prev, b_up, b_down), "section", 2)
    highs = keep_high(highs, b_up, (z + 6) % 8, 0)
    highs = keep_high(highs, b_down, (z + 2) % 8, 0)
    b_up, b_down = shift(b_up, "z", 1), shift(b_down, "z", -1)
    highs = keep_high(highs, b_up, (z + 5) % 8, 0)
    highs = keep_high(highs, b_down, (z + 3) % 8, 0)
    a_up, a_down = shift(a_up[:4], "y", 1), shift(a_down[4:], "y", -1)
    lows = keep_low(lows, a_up, 0, (y + 2) % 4)
    lows = keep_low(lows, a_down, 4, (y + 2) % 4)
    b_up, b_down = shift(b_up[:2], "z", 1), shift(b_down[2:], "z", -1)
    highs = keep_high(highs, b_up, (z + 4) % 8, 0)
    highs = keep_high(highs, b_down, (z + 4) % 8, 2)
    late_y = after(late_y, b_up, b_down, a_up, a_down)
    lows, highs = (lows[0], lows[1].reshape(-1, 512, 512)), (highs[0], highs[1].reshape(-1, 512, 512))
    return lows[0], highs[0], lows[1], highs[1], late_y, segs


def project_kernel(rows, gain, key_hbm, value_hbm, out, key_w, value_w, sems):
    copies = []
    for n in range(CHUNKS):
        part = pl.ds(DEPTH * n, DEPTH)
        copies.append(
            (
                pltpu.make_async_copy(key_hbm.at[part], key_w.at[part], sems.at[2 * n]),
                pltpu.make_async_copy(value_hbm.at[part], value_w.at[part], sems.at[2 * n + 1]),
            )
        )
    for pair in copies:
        for copy in pair:
            copy.start()
    many = rows.shape[0]
    key_sum = jnp.zeros((many, 512), F32)
    value_sum = jnp.zeros((many, 512), F32)
    squares = jnp.zeros((many, 1), F32)
    for n in range(CHUNKS):
        cols = slice(n * WIDTH, n * WIDTH + WIDTH)
        part = slice(DEPTH * n, DEPTH * n + DEPTH)
        wide = rows[:, cols].astype(F32)
        squares = squares + jnp.sum(wide * wide, axis=1, keepdims=True)
        scaled = (wide * gain[:, cols].astype(F32)).astype(BF16)
        copies[n][0].wait()
        key_sum += jnp.dot(scaled, key_w[part].reshape(WIDTH, 512), preferred_element_type=F32)
        copies[n][1].wait()
        value_sum += jnp.dot(scaled, value_w[part].reshape(WIDTH, 512), preferred_element_type=F32)
    out[:, :512] = key_sum
    out[:, 512:1024] = value_sum
    out[:, 1024:] = jnp.broadcast_to(squares, (many, 128))


def project(rows, gain, w_key, w_value):
    return pl.pallas_call(
        project_kernel,
        out_shape=jax.ShapeDtypeStruct((rows.shape[0], 1152), F32),
        in_specs=[VMEM, VMEM, ANY, ANY],
        out_specs=VMEM,
        scratch_shapes=[
            pltpu.VMEM((8, 4, 128, 512), BF16),
            pltpu.VMEM((8, 4, 128, 512), BF16),
            pltpu.SemaphoreType.DMA((2 * CHUNKS,)),
        ],
        compiler_params=pltpu.CompilerParams(vmem_limit_bytes=12 * 2**20),
        cost_estimate=pl.CostEstimate(
            flops=2 * rows.shape[0] * HALF * 1024, bytes_accessed=8 * 2**20, transcendentals=0
        ),
        name="project",
    )(rows, gain, w_key, w_value)


def attend_kernel(start, stop, joined, *refs):
    refs = list(refs)
    own, other_hbm, seg = refs[:3]
    del refs[:3]
    earlier = refs.pop(0) if start else None
    begun = refs.pop(0) if joined else None
    out = refs.pop(0)
    kept = refs.pop(0) if stop < ROWS else None
    other, sem = refs
    copy = pltpu.make_async_copy(other_hbm, other, sem)
    copy.start()
    i = lax.broadcasted_iota(jnp.int32, (ROWS, ROWS), 0)
    j = lax.broadcasted_iota(jnp.int32, (ROWS, ROWS), 1)
    wide = jnp.broadcast_to(seg[...].astype(F32), (ROWS, ROWS))
    bias = jnp.where((j <= i) & (wide == wide.T), 0.0, 1.0)[start:stop, :stop]
    copy.wait()
    squares = own[:, 1024:1025] + other[:, 1024:1025]
    scale = lax.rsqrt(squares / D + 1e-05)
    both = ((own[:, :1024] + other[:, :1024]) * scale).astype(BF16)
    if kept is not None:
        kept[...] = both
    if joined:
        out[:start, :] = begun[...]
    cols = [slice(head * HD, head * HD + HD) for head in range(4)]
    every = both if earlier is None else jnp.concatenate([earlier[...], both], axis=0)
    scores = [
        lax.dot_general(
            both[:, c], every[:, c], (((1,), (1,)), ((), ())), preferred_element_type=F32
        )
        / HD
        for c in cols
    ]
    scores = [jnp.where(bias == 0.0, each, -1e30) for each in scores]
    lifted = [jnp.exp(each - jnp.max(each, axis=1, keepdims=True)) for each in scores]
    probs = [(each / jnp.sum(each, axis=1, keepdims=True)).astype(BF16) for each in lifted]
    shift_by = start if joined else 0
    for c, each in zip(cols, probs):
        values = every[:, 512 + c.start : 512 + c.stop]
        found = jnp.dot(each, values, preferred_element_type=F32).astype(BF16)
        out[shift_by : shift_by + stop - start, c] = found


def attend(own, seg, start, stop, earlier=None, begun=None):
    joined = begun is not None
    many = stop - start
    shapes = [jax.ShapeDtypeStruct((stop if joined else many, 512), BF16)]
    if stop < ROWS:
        shapes.append(jax.ShapeDtypeStruct((many, 1024), BF16))
    extra = [each for each in (earlier, begun) if each is not None]
    return pl.pallas_call(
        functools.partial(attend_kernel, start, stop, joined),
        out_shape=shapes,
        in_specs=[VMEM, ANY, VMEM] + [VMEM] * len(extra),
        out_specs=[VMEM] * len(shapes),
        scratch_shapes=[pltpu.VMEM((many, 1152), F32), pltpu.SemaphoreType.DMA],
        compiler_params=pltpu.CompilerParams(vmem_limit_bytes=4 * 2**20),
        name="attend",
    )(own, shift(own, "tensor", 1), seg, *extra)


def mix_kernel(places, split, *refs):
    sources = refs[: 1 + max(which for which, _ in places)]
    refs = refs[len(sources) :]
    heads, rows, outs, held, sems = refs[0], refs[1], refs[2 : 2 + split], refs[-2], refs[-1]
    copies = [
        pltpu.make_async_copy(sources[which].at[index], held.at[n], sems.at[n])
        for n, (which, index) in enumerate(places)
    ]
    for copy in copies:
        copy.start()
    many = rows.shape[0] // split
    for n, copy in enumerate(copies):
        cols = slice(n * 512, n * 512 + 512)
        copy.wait()
        mixed = jnp.dot(heads[...], held[n], preferred_element_type=F32)
        mixed = (rows[:, cols].astype(F32) + mixed).astype(BF16)
        for part, out in enumerate(outs):
            out[:, cols] = mixed[part * many : part * many + many]


def mix(weights, heads, rows, split=1):
    sources = []
    places = []
    for array, index in weights:
        found = [n for n, other in enumerate(sources) if other is array]
        if not found:
            sources.append(array)
        places.append((found[0] if found else len(sources) - 1, index))
    shape = jax.ShapeDtypeStruct((rows.shape[0] // split, HALF), BF16)
    return pl.pallas_call(
        functools.partial(mix_kernel, tuple(places), split),
        out_shape=[shape] * split,
        in_specs=[ANY] * len(sources) + [VMEM, VMEM],
        out_specs=[VMEM] * split,
        scratch_shapes=[pltpu.VMEM((8, 512, 512), BF16), pltpu.SemaphoreType.DMA((8,))],
        compiler_params=pltpu.CompilerParams(vmem_limit_bytes=8 * 2**20),
        cost_estimate=pl.CostEstimate(
            flops=2 * rows.shape[0] * 512 * HALF, bytes_accessed=2**22, transcendentals=0
        ),
        name="mix",
    )(*sources, heads, rows)


class Late:
    def __init__(self, own):
        z = lax.axis_index("z")
        self.z, self.up, self.down, self.step = z, own, own, 0
        self.held = jnp.zeros((8, 8, 4, 16, 512), BF16)
        self.keep(own, 0, 0)

    def keep(self, block, offset, first):
        part = block.reshape(block.shape[0], 8, 16, 512).transpose(1, 0, 2, 3)
        self.held = place(self.held, part[:, None], 0, (self.z + offset) % 8, first)

    def advance(self, *earlier):
        self.step += 1
        up, down = after(self.up, *earlier), after(self.down, *earlier)
        if self.step < 4:
            self.up, self.down = shift(up, "z", 1), shift(down, "z", -1)
            self.keep(self.up, 8 - self.step, 0)
            self.keep(self.down, self.step, 0)
        else:
            self.keep(shift(up[:2], "z", 1), 4, 0)
            self.keep(shift(down[2:], "z", -1), 4, 2)

    def blocks(self):
        return self.held.reshape(8, 512, 512)


def per_device(inputs, segment_ids, key_weight, value_weight, out_weight, norm_gain):
    x_part = inputs[0]
    core = lax.axis_index("tensor")
    gain = lax.dynamic_slice(norm_gain, (0, core * HALF), (1, HALF))
    w_next = blocks_of(shift(out_weight[0], "section", -1))
    seg = segment_ids
    w_key, w_value, out_low, out_high, late_y, (seg_prev, seg_prev2) = gather_weights(
        key_weight[0], value_weight[0], out_weight[0], w_next, seg
    )
    late = Late(late_y)
    own = [(out_low, n) if n < LOW else (out_high, n - LOW) for n in range(8)]

    def sums(rows):
        return project(rows, gain, w_key, w_value)

    (heads,) = attend(sums(after(x_part, seg_prev, seg_prev2)), seg, 0, ROWS)
    first = mix(own, heads, x_part, 2)
    late.advance()
    one = late.up, late.down
    late.advance(*first)
    two = late.up, late.down
    first = [shift(part, "section", 1) for part in first]
    heads, kept = attend(sums(after(first[0], *one)), seg_prev, 0, 64)
    final = mix(own, heads, first[0])
    moved = [shift(final[0], "section", 1)]
    (heads,) = attend(sums(after(first[1], final[0], *two)), seg_prev, 64, ROWS, kept)
    final += mix(own, heads, first[1])
    moved.append(shift(final[1], "section", 1))
    late.advance()
    late.advance(final[1])
    begun, kept = attend(sums(moved[0]), seg_prev2, 0, 64)
    (heads,) = attend(sums(after(moved[1], begun)), seg_prev2, 64, ROWS, kept, begun)
    heads = shift(heads, "section", -1)
    final = jnp.concatenate(final, axis=0)
    following = late.blocks()
    (backup,) = mix([(following, n) for n in range(8)], heads, final)
    return (final[None], backup[None])


def solution(mesh):
    fine = Mesh(mesh.devices.reshape(4, 2, 8, 4), ("section", "tensor", "z", "y"))
    dp = ("z", "y")
    in_specs = (
        P("section", dp, "tensor"),
        P("section", dp),
        P("section", ("tensor",) + dp, None),
        P("section", ("tensor",) + dp, None),
        P("section", dp, "tensor"),
        P("section", None),
    )
    out_specs = (P("section", dp, "tensor"), P("section", dp, "tensor"))
    return jax.shard_map(
        per_device, mesh=fine, in_specs=in_specs, out_specs=out_specs, check_vma=False
    )
```

```python
import functools

import jax
import jax.numpy as jnp
from jax import lax
from jax.experimental import pallas as pl
from jax.experimental.pallas import tpu as pltpu
from jax.sharding import Mesh
from jax.sharding import PartitionSpec as P

D = 8192
HD = 128
ROWS = 128
HALF = 4096
CHUNKS = 4
WIDTH = HALF // CHUNKS
DEPTH = 8 // CHUNKS
LOW = 5
F32 = jnp.float32
BF16 = jnp.bfloat16
ANY = pl.BlockSpec(memory_space=pl.ANY)
VMEM = pl.BlockSpec(memory_space=pltpu.VMEM)


def shift(block, axis, distance):
    n = lax.axis_size(axis)
    return lax.ppermute(block, axis, [(i, (i + distance) % n) for i in range(n)])


def place(buffer, block, *where):
    start = list(where) + [0] * (buffer.ndim - len(where))
    return lax.dynamic_update_slice(buffer, block, start)


def after(block, *earlier):
    return lax.optimization_barrier((block,) + earlier)[0]


def blocks_of(w_out):
    return w_out.reshape(16, 8, 512).transpose(1, 0, 2).reshape(128, 512)


def gather_weights(w_key, w_value, w_out, w_late, seg):
    z, y = lax.axis_index("z"), lax.axis_index("y")
    w_out = blocks_of(w_out)
    low = jnp.concatenate([w_key, w_out[: LOW * 16]], axis=0)
    high = jnp.concatenate([w_value, w_out[LOW * 16 :], w_late], axis=0)
    n_low, n_high, n_soon = 128 + LOW * 16, 384 - LOW * 16, 256 - LOW * 16
    h_low, h_high = n_low // 2, n_high // 2

    low_up, low_down = shift(low, "z", 1), shift(low, "z", -1)
    high = after(high, low_up, low_down)
    high_up, high_down = shift(high, "y", 1), shift(high, "y", -1)
    low_z = place(place(jnp.zeros((8, n_low, 512), BF16), low_up[None], (z + 7) % 8), low_down[None], (z + 1) % 8)
    low_z = place(low_z, low[None], z)
    high_y = place(place(jnp.zeros((4, n_high, 512), BF16), high_up[None], (y + 3) % 4), high_down[None], (y + 1) % 4)
    high_y = place(high_y, high[None], y)
    up2 = shift(low_up, "z", 1)
    down2 = shift(low_down, "z", -1)
    low_z = place(place(low_z, up2[None], (z + 6) % 8), down2[None], (z + 2) % 8)
    far_up = shift(after(high_up[:h_high], up2, down2), "y", 1)
    far_down = shift(after(high_down[h_high:], up2, down2), "y", -1)
    high_y = place(place(high_y, far_up[None], (y + 2) % 4), far_down[None], (y + 2) % 4, h_high)
    up3 = shift(up2, "z", 1)
    down3 = shift(down2, "z", -1)
    low_z = place(place(low_z, up3[None], (z + 5) % 8), down3[None], (z + 3) % 8)
    late_y = high_y[:, n_soon:]
    high_y = after(high_y[:, :n_soon], up3, down3)
    up4, down4 = shift(up3[:h_low], "z", 1), shift(down3[h_low:], "z", -1)
    low_z = place(place(low_z, up4[None], (z + 4) % 8), down4[None], (z + 4) % 8, h_low)

    key = jnp.zeros((8, 4, 128, 512), BF16)
    value = jnp.zeros((8, 4, 128, 512), BF16)
    out_low = jnp.zeros((LOW, 8, 4, 16, 512), BF16)
    out_high = jnp.zeros((8 - LOW, 8, 4, 16, 512), BF16)

    def keep_low(buffers, block, first, at):
        key, out = buffers
        many = block.shape[0]
        part = block[:, 128:].reshape(many, -1, 16, 512).transpose(1, 0, 2, 3)
        return (
            place(key, block[:, None, :128], first, at),
            place(out, part[:, :, None], 0, first, at),
        )

    def keep_high(buffers, block, at, first):
        value, out = buffers
        many = block.shape[0]
        part = block[:, 128:].reshape(many, -1, 16, 512).transpose(1, 0, 2, 3)
        return (
            place(value, block[None, :, :128], at, first),
            place(out, part[:, None], 0, at, first),
        )

    lows = keep_low((key, out_low), low_z, 0, y)
    highs = keep_high((value, out_high), high_y, z, 0)
    b_up, b_down = shift(high_y, "z", 1), shift(high_y, "z", -1)
    a_up, a_down = shift(low_z, "y", 1), shift(low_z, "y", -1)
    lows = keep_low(lows, a_up, 0, (y + 3) % 4)
    lows = keep_low(lows, a_down, 0, (y + 1) % 4)
    prev = shift(after(seg, b_up, b_down), "section", 1)
    highs = keep_high(highs, b_up, (z + 7) % 8, 0)
    highs = keep_high(highs, b_down, (z + 1) % 8, 0)
    b_up, b_down = shift(after(b_up, up4), "z", 1), shift(after(b_down, down4), "z", -1)
    segs = prev, shift(after(seg, prev, b_up, b_down), "section", 2)
    highs = keep_high(highs, b_up, (z + 6) % 8, 0)
    highs = keep_high(highs, b_down, (z + 2) % 8, 0)
    b_up, b_down = shift(b_up, "z", 1), shift(b_down, "z", -1)
    highs = keep_high(highs, b_up, (z + 5) % 8, 0)
    highs = keep_high(highs, b_down, (z + 3) % 8, 0)
    a_up, a_down = shift(a_up[:4], "y", 1), shift(a_down[4:], "y", -1)
    lows = keep_low(lows, a_up, 0, (y + 2) % 4)
    lows = keep_low(lows, a_down, 4, (y + 2) % 4)
    b_up, b_down = shift(b_up[:2], "z", 1), shift(b_down[2:], "z", -1)
    highs = keep_high(highs, b_up, (z + 4) % 8, 0)
    highs = keep_high(highs, b_down, (z + 4) % 8, 2)
    late_y = after(late_y, b_up, b_down, a_up, a_down)
    lows, highs = (lows[0], lows[1].reshape(-1, 512, 512)), (highs[0], highs[1].reshape(-1, 512, 512))
    return lows[0], highs[0], lows[1], highs[1], late_y, segs


def project_kernel(rows, gain, key_hbm, value_hbm, out, key_w, value_w, sems):
    copies = []
    for n in range(CHUNKS):
        part = pl.ds(DEPTH * n, DEPTH)
        copies.append(
            (
                pltpu.make_async_copy(key_hbm.at[part], key_w.at[part], sems.at[2 * n]),
                pltpu.make_async_copy(value_hbm.at[part], value_w.at[part], sems.at[2 * n + 1]),
            )
        )
    for pair in copies:
        for copy in pair:
            copy.start()
    many = rows.shape[0]
    key_sum = jnp.zeros((many, 512), F32)
    value_sum = jnp.zeros((many, 512), F32)
    squares = jnp.zeros((many, 1), F32)
    for n in range(CHUNKS):
        cols = slice(n * WIDTH, n * WIDTH + WIDTH)
        part = slice(DEPTH * n, DEPTH * n + DEPTH)
        wide = rows[:, cols].astype(F32)
        squares = squares + jnp.sum(wide * wide, axis=1, keepdims=True)
        scaled = (wide * gain[:, cols].astype(F32)).astype(BF16)
        copies[n][0].wait()
        key_sum += jnp.dot(scaled, key_w[part].reshape(WIDTH, 512), preferred_element_type=F32)
        copies[n][1].wait()
        value_sum += jnp.dot(scaled, value_w[part].reshape(WIDTH, 512), preferred_element_type=F32)
    out[:, :512] = key_sum
    out[:, 512:1024] = value_sum
    out[:, 1024:] = jnp.broadcast_to(squares, (many, 128))


def project(rows, gain, w_key, w_value):
    return pl.pallas_call(
        project_kernel,
        out_shape=jax.ShapeDtypeStruct((rows.shape[0], 1152), F32),
        in_specs=[VMEM, VMEM, ANY, ANY],
        out_specs=VMEM,
        scratch_shapes=[
            pltpu.VMEM((8, 4, 128, 512), BF16),
            pltpu.VMEM((8, 4, 128, 512), BF16),
            pltpu.SemaphoreType.DMA((2 * CHUNKS,)),
        ],
        compiler_params=pltpu.CompilerParams(vmem_limit_bytes=12 * 2**20),
        cost_estimate=pl.CostEstimate(
            flops=2 * rows.shape[0] * HALF * 1024, bytes_accessed=8 * 2**20, transcendentals=0
        ),
        name="project",
    )(rows, gain, w_key, w_value)


def attend_kernel(start, stop, joined, *refs):
    refs = list(refs)
    own, other_hbm, seg = refs[:3]
    del refs[:3]
    earlier = refs.pop(0) if start else None
    begun = refs.pop(0) if joined else None
    out = refs.pop(0)
    kept = refs.pop(0) if stop < ROWS else None
    other, sem = refs
    copy = pltpu.make_async_copy(other_hbm, other, sem)
    copy.start()
    i = lax.broadcasted_iota(jnp.int32, (ROWS, ROWS), 0)
    j = lax.broadcasted_iota(jnp.int32, (ROWS, ROWS), 1)
    wide = jnp.broadcast_to(seg[...].astype(F32), (ROWS, ROWS))
    bias = jnp.where((j <= i) & (wide == wide.T), 0.0, 1.0)[start:stop, :stop]
    copy.wait()
    squares = own[:, 1024:1025] + other[:, 1024:1025]
    scale = lax.rsqrt(squares / D + 1e-05)
    both = ((own[:, :1024] + other[:, :1024]) * scale).astype(BF16)
    if kept is not None:
        kept[...] = both
    if joined:
        out[:start, :] = begun[...]
    cols = [slice(head * HD, head * HD + HD) for head in range(4)]
    every = both if earlier is None else jnp.concatenate([earlier[...], both], axis=0)
    scores = [
        lax.dot_general(
            both[:, c], every[:, c], (((1,), (1,)), ((), ())), preferred_element_type=F32
        )
        / HD
        for c in cols
    ]
    scores = [jnp.where(bias == 0.0, each, -1e30) for each in scores]
    lifted = [jnp.exp(each - jnp.max(each, axis=1, keepdims=True)) for each in scores]
    probs = [(each / jnp.sum(each, axis=1, keepdims=True)).astype(BF16) for each in lifted]
    shift_by = start if joined else 0
    for c, each in zip(cols, probs):
        values = every[:, 512 + c.start : 512 + c.stop]
        found = jnp.dot(each, values, preferred_element_type=F32).astype(BF16)
        out[shift_by : shift_by + stop - start, c] = found


def attend(own, seg, start, stop, earlier=None, begun=None):
    joined = begun is not None
    many = stop - start
    shapes = [jax.ShapeDtypeStruct((stop if joined else many, 512), BF16)]
    if stop < ROWS:
        shapes.append(jax.ShapeDtypeStruct((many, 1024), BF16))
    extra = [each for each in (earlier, begun) if each is not None]
    return pl.pallas_call(
        functools.partial(attend_kernel, start, stop, joined),
        out_shape=shapes,
        in_specs=[VMEM, ANY, VMEM] + [VMEM] * len(extra),
        out_specs=[VMEM] * len(shapes),
        scratch_shapes=[pltpu.VMEM((many, 1152), F32), pltpu.SemaphoreType.DMA],
        compiler_params=pltpu.CompilerParams(vmem_limit_bytes=4 * 2**20),
        name="attend",
    )(own, shift(own, "tensor", 1), seg, *extra)


def mix_kernel(places, split, *refs):
    sources = refs[: 1 + max(which for which, _ in places)]
    refs = refs[len(sources) :]
    heads, rows, outs, held, sems = refs[0], refs[1], refs[2 : 2 + split], refs[-2], refs[-1]
    copies = [
        pltpu.make_async_copy(sources[which].at[index], held.at[n], sems.at[n])
        for n, (which, index) in enumerate(places)
    ]
    for copy in copies:
        copy.start()
    many = rows.shape[0] // split
    for n, copy in enumerate(copies):
        cols = slice(n * 512, n * 512 + 512)
        copy.wait()
        mixed = jnp.dot(heads[...], held[n], preferred_element_type=F32)
        mixed = (rows[:, cols].astype(F32) + mixed).astype(BF16)
        for part, out in enumerate(outs):
            out[:, cols] = mixed[part * many : part * many + many]


def mix(weights, heads, rows, split=1):
    sources = []
    places = []
    for array, index in weights:
        found = [n for n, other in enumerate(sources) if other is array]
        if not found:
            sources.append(array)
        places.append((found[0] if found else len(sources) - 1, index))
    shape = jax.ShapeDtypeStruct((rows.shape[0] // split, HALF), BF16)
    return pl.pallas_call(
        functools.partial(mix_kernel, tuple(places), split),
        out_shape=[shape] * split,
        in_specs=[ANY] * len(sources) + [VMEM, VMEM],
        out_specs=[VMEM] * split,
        scratch_shapes=[pltpu.VMEM((8, 512, 512), BF16), pltpu.SemaphoreType.DMA((8,))],
        compiler_params=pltpu.CompilerParams(vmem_limit_bytes=8 * 2**20),
        cost_estimate=pl.CostEstimate(
            flops=2 * rows.shape[0] * 512 * HALF, bytes_accessed=2**22, transcendentals=0
        ),
        name="mix",
    )(*sources, heads, rows)


class Late:
    def __init__(self, own):
        z = lax.axis_index("z")
        self.z, self.up, self.down, self.step = z, own, own, 0
        self.held = jnp.zeros((8, 8, 4, 16, 512), BF16)
        self.keep(own, 0, 0)

    def keep(self, block, offset, first):
        part = block.reshape(block.shape[0], 8, 16, 512).transpose(1, 0, 2, 3)
        self.held = place(self.held, part[:, None], 0, (self.z + offset) % 8, first)

    def advance(self, *earlier):
        self.step += 1
        up, down = after(self.up, *earlier), after(self.down, *earlier)
        if self.step < 4:
            self.up, self.down = shift(up, "z", 1), shift(down, "z", -1)
            self.keep(self.up, 8 - self.step, 0)
            self.keep(self.down, self.step, 0)
        else:
            self.keep(shift(up[:2], "z", 1), 4, 0)
            self.keep(shift(down[2:], "z", -1), 4, 2)

    def blocks(self):
        return self.held.reshape(8, 512, 512)


def per_device(inputs, segment_ids, key_weight, value_weight, out_weight, norm_gain):
    x_part = inputs[0]
    core = lax.axis_index("tensor")
    gain = lax.dynamic_slice(norm_gain, (0, core * HALF), (1, HALF))
    w_next = blocks_of(shift(out_weight[0], "section", -1))
    seg = segment_ids
    w_key, w_value, out_low, out_high, late_y, (seg_prev, seg_prev2) = gather_weights(
        key_weight[0], value_weight[0], out_weight[0], w_next, seg
    )
    late = Late(late_y)
    own = [(out_low, n) if n < LOW else (out_high, n - LOW) for n in range(8)]

    def sums(rows):
        return project(rows, gain, w_key, w_value)

    (heads,) = attend(sums(after(x_part, seg_prev, seg_prev2)), seg, 0, ROWS)
    first = mix(own, heads, x_part, 2)
    late.advance(*first)
    one = late.up, late.down
    late.advance()
    two = late.up, late.down
    first = [shift(part, "section", 1) for part in first]
    heads, kept = attend(sums(after(first[0], *one)), seg_prev, 0, 64)
    final = mix(own, heads, first[0])
    moved = [shift(final[0], "section", 1)]
    (heads,) = attend(sums(after(first[1], final[0], *two)), seg_prev, 64, ROWS, kept)
    final += mix(own, heads, first[1])
    moved.append(shift(final[1], "section", 1))
    late.advance()
    late.advance(final[1])
    begun, kept = attend(sums(moved[0]), seg_prev2, 0, 64)
    (heads,) = attend(sums(after(moved[1], begun)), seg_prev2, 64, ROWS, kept, begun)
    heads = shift(heads, "section", -1)
    final = jnp.concatenate(final, axis=0)
    following = late.blocks()
    (backup,) = mix([(following, n) for n in range(8)], heads, final)
    return (final[None], backup[None])


def solution(mesh):
    fine = Mesh(mesh.devices.reshape(4, 2, 8, 4), ("section", "tensor", "z", "y"))
    dp = ("z", "y")
    in_specs = (
        P("section", dp, "tensor"),
        P("section", dp),
        P("section", ("tensor",) + dp, None),
        P("section", ("tensor",) + dp, None),
        P("section", dp, "tensor"),
        P("section", None),
    )
    out_specs = (P("section", dp, "tensor"), P("section", dp, "tensor"))
    return jax.shard_map(
        per_device, mesh=fine, in_specs=in_specs, out_specs=out_specs, check_vma=False
    )
```
